32 devices in a mesh: fsdp: 8 (over z, x), ctx: 2 (over y), tp: 2 (over core).
Axes of the slice: x: 2, y: 2, z: 4, core: 2. Of those that a mesh axis runs over, the one named last changes fastest.
Arguments:
- block_in: bfloat16 [8, 1024, 2048], P('fsdp', 'ctx'), may hold values from -36 to 36
- segments: int32 [8, 1024], P('fsdp', 'ctx'), may hold values from 0 to 3, as said below
- positions: int32 [8, 1024], P('fsdp', 'ctx'), may hold values from 0 to 3071, as said below
- gain_one: bfloat16 [2048], replicated, may hold values from 0.099609375 to 1.8984375
- shift_one: bfloat16 [2048], replicated, may hold values from -3 to 3
- qkv_weight: bfloat16 [2048, 3, 2048], P('fsdp', None, 'tp'), may hold values from -0.125 to 0.125
- qkv_bias: bfloat16 [3, 32, 64], P(None, 'tp'), may hold values from -3 to 3
- out_weight: bfloat16 [2048, 2048], P('fsdp', 'tp'), may hold values from -0.5 to 0.5
- gain_two: bfloat16 [2048], replicated, may hold values from 0.099609375 to 1.8984375
- shift_two: bfloat16 [2048], replicated, may hold values from -3 to 3
- gate_weight: bfloat16 [2048, 5632], P('fsdp', 'tp'), may hold values from -0.125 to 0.125
- up_weight: bfloat16 [2048, 5632], P('fsdp', 'tp'), may hold values from -0.125 to 0.125
- down_weight: bfloat16 [2048, 5632], P('fsdp', 'tp'), may hold values from -0.15625 to 0.15625
- grad_out: bfloat16 [8, 1024, 2048], P('fsdp', 'ctx'), may hold values from -6 to 6
Outputs:
- block_out: bfloat16 [8, 1024, 2048], P('fsdp', 'ctx')
- grad_in: float32 [8, 1024, 2048], P('fsdp', 'ctx')
- grad_gain_one: float32 [2048], P(('fsdp', 'ctx'))
- grad_shift_one: float32 [2048], P(('fsdp', 'ctx'))
- grad_qkv_weight: float32 [2048, 3, 2048], P(('fsdp', 'ctx'), None, 'tp')
- grad_qkv_bias: float32 [3, 32, 64], P(None, 'tp', ('fsdp', 'ctx'))
- grad_out_weight: float32 [2048, 2048], P(('fsdp', 'ctx'), 'tp')
- grad_gain_two: float32 [2048], P(('fsdp', 'ctx'))
- grad_shift_two: float32 [2048], P(('fsdp', 'ctx'))
- grad_gate_weight: float32 [2048, 5632], P(('fsdp', 'ctx'), 'tp')
- grad_up_weight: float32 [2048, 5632], P(('fsdp', 'ctx'), 'tp')
- grad_down_weight: float32 [2048, 5632], P(('fsdp', 'ctx'), 'tp')
The draws below stay inside these ranges and needn't reach their ends.
Inputs may be any that keep to these rules, and one draw needn't show every extreme that they name: `segments`: each sequence holds four documents numbered 0 to 3 in order, each of one token or more; document 1 starts at a token index from 1 to 128 and its last token has an index from 895 to 1021. Within a document the positions count up by one from its first token; document 0 of every sequence starts at 0, documents 1 and 2 at a start below 2048, and document 3 ends at 3071.
All inputs are finite; a program needn't handle non-finite values.
Results may differ from the reference program's by a relative error of at most 0.017.
Values may be sent and summed in bfloat16 or wider, within the bound.
A program may use at most 320 MiB of HBM per device.

```python
import math
import jax
import jax.numpy as jnp
from jax import lax

D = 2048
H = 32
HD = 64
FF = 5632
ROT = 16
LEN = 1024
SEQ = 8


def document_bounds(key):
    first_key, second_key, third_key = jax.random.split(key, 3)
    first_cut = jax.random.randint(first_key, (SEQ, 1), 1, LEN // 8 + 1)
    second_cut = jax.random.randint(second_key, (SEQ, 1), LEN - LEN // 8, LEN - 1)
    third_cut = jax.random.randint(third_key, (SEQ, 1), second_cut + 1, LEN)
    return (first_cut, second_cut, third_cut)


def segment_of(cuts):
    place = jnp.arange(LEN, dtype=jnp.int32)[None, :]
    return (place >= cuts[0]).astype(jnp.int32) + (place >= cuts[1]).astype(jnp.int32) + (place >= cuts[2]).astype(jnp.int32)


def draw_segments(key, part):
    cuts = document_bounds(key)
    return segment_of(cuts)


def draw_positions(key, part):
    cuts = document_bounds(key)
    key = jax.random.fold_in(key, 7)
    starts = jax.random.randint(key, (SEQ, 2), 0, 2 * LEN)
    segment = segment_of(cuts)
    place = jnp.arange(LEN, dtype=jnp.int32)[None, :]
    last_anchor = 2 * LEN + cuts[2]
    begin = jnp.where(segment == 1, cuts[0], jnp.where(segment == 2, cuts[1], jnp.where(segment == 3, cuts[2], 0)))
    anchor = jnp.where(segment == 1, starts[:, 0:1], jnp.where(segment == 2, starts[:, 1:2], jnp.where(segment == 3, last_anchor, 0)))
    return (anchor + place - begin).astype(jnp.int32)


def draw_block_in(key, part):
    key = jax.random.fold_in(key, 11)
    row_key, col_key, base_key = jax.random.split(key, 3)
    row_scale = jnp.exp(jax.random.uniform(row_key, (SEQ, LEN, 1), minval=math.log(0.3), maxval=math.log(3.0)))
    col_scale = jnp.exp(jax.random.uniform(col_key, (1, 1, D), minval=math.log(0.3), maxval=math.log(3.0)))
    base = jax.random.normal(base_key, (SEQ, LEN, D))
    base = jnp.clip(base, -4.0, 4.0)
    return (base * row_scale * col_scale).astype(jnp.bfloat16)


def raised(drawn, stream_key, source, target, shards_of, factor):
    def block_of(axis_at):
        return (jnp.arange(drawn.shape[axis_at]) // (drawn.shape[axis_at] // shards_of)).reshape((-1,) + (1,) * (drawn.ndim - 1 - axis_at))

    first = jax.random.permutation(stream_key, shards_of)[block_of(target)]
    far = (block_of(target) + shards_of // 2) % shards_of
    return jnp.where((block_of(source) == first) | (block_of(source) == far), factor * drawn, drawn)


def level_of(stream_key, shape, pieces, smallest, high):
    level = 1.0
    for dim, parts in pieces:
        heights = jax.random.uniform(jax.random.fold_in(jax.random.fold_in(stream_key, 6), dim), (parts,), jnp.float32, smallest / len(pieces), high / len(pieces))
        level = level * jnp.repeat(jnp.exp(heights), shape[dim] // parts).reshape((-1,) + (1,) * (len(shape) - 1 - dim))
    return level


def scatter_about(key, shape, spread, bound, pieces=(), held_as=jnp.bfloat16):
    factor_of = level_of(key, shape, pieces, -0.22, 0.18) if pieces else 1.0
    array = jax.random.normal(key, shape, jnp.float32) * spread * factor_of
    return jnp.minimum(jnp.maximum(array, -bound), bound).astype(held_as)


def noise_with(key, shape, scale, limit, shards, heavy, kind=jnp.bfloat16):
    array = scale * jax.random.normal(key, shape, jnp.float32)
    if shards:
        array = array * level_of(key, shape, shards, -0.22, 0.18)
    return jnp.clip(raised(array, jax.random.fold_in(key, 3), *heavy), -limit, limit).astype(kind)


def setup_inputs(seed: int = 0) -> dict:
    arg_keys = jax.random.split(jax.random.key(seed), 15)
    return {
        "block_in": draw_block_in(jax.random.fold_in(arg_keys[14], 71), 0),
        "segments": draw_segments(jax.random.fold_in(arg_keys[14], 71), 0),
        "positions": draw_positions(jax.random.fold_in(arg_keys[14], 71), 0),
        "gain_one": jnp.clip(1.0 + 0.18 * jax.random.normal(arg_keys[3], (D,), jnp.float32), 0.099609375, 1.8984375).astype(jnp.bfloat16),
        "shift_one": scatter_about(arg_keys[4], (D,), 0.5, 3.0),
        "qkv_weight": scatter_about(arg_keys[5], (D, 3, D), D ** -0.5, 0.125, ((0, 8), (2, 2))),
        "qkv_bias": scatter_about(arg_keys[6], (3, H, HD), 0.5, 3.0, ((1, 2),)),
        "out_weight": scatter_about(arg_keys[7], (D, D), (D // 16) ** -0.5, 0.5, ((0, 8), (1, 2))),
        "gain_two": jnp.clip(1.0 + 0.18 * jax.random.normal(arg_keys[8], (D,), jnp.float32), 0.099609375, 1.8984375).astype(jnp.bfloat16),
        "shift_two": scatter_about(arg_keys[9], (D,), 0.5, 3.0),
        "gate_weight": scatter_about(arg_keys[10], (D, FF), D ** -0.5, 0.125, ((0, 8), (1, 2))),
        "up_weight": scatter_about(arg_keys[11], (D, FF), D ** -0.5, 0.125, ((0, 8), (1, 2))),
        "down_weight": scatter_about(arg_keys[12], (D, FF), (FF // 4) ** -0.5, 0.15625, ((0, 8), (1, 2))),
        "grad_out": noise_with(arg_keys[13], (SEQ, LEN, D), 1.0, 6.0, ((0, 8), (1, 2)), (0, 2, 8, 2.0)),
    }


epsilon = 1e-05
theta_base = 10000.0
masked_value = -1e+30

@jax.custom_vjp
def low(v):
    return lax.optimization_barrier(v.astype(jnp.bfloat16)).astype(jnp.float32)

@jax.custom_vjp
def low_back(v):
    return v

def low_keep(v):
    return (low(v), None)

def low_pass(kept, grad):
    return (grad,)

def back_keep(v):
    return (v, None)

def back_low(kept, grad):
    return (low(grad),)
low.defvjp(low_keep, low_pass)
low_back.defvjp(back_keep, back_low)

def matmul(left, right):
    return jnp.dot(left, right, precision=lax.Precision.HIGHEST, preferred_element_type=jnp.float32)

def normalize(source, gain_vec, offset):
    average = lax.optimization_barrier(jnp.mean(source, axis=-1, keepdims=True))
    centered = source - average
    inv_std = lax.rsqrt(lax.optimization_barrier(jnp.mean(centered * centered, axis=-1, keepdims=True)) + epsilon)
    return centered * inv_std * gain_vec + offset

def rotation(positions, rotary):
    half_dims = rotary // 2
    frequency = theta_base ** (-(2.0 * jnp.arange(half_dims, dtype=jnp.float32)) / rotary)
    angles = positions.astype(jnp.float32)[..., None] * frequency
    return (jnp.cos(angles), jnp.sin(angles))

def turn(source, cosine, sine_part, rotary):
    half_dims = rotary // 2
    first_half = source[..., :half_dims]
    second = source[..., half_dims:rotary]
    return jnp.concatenate([first_half * cosine - second * sine_part, second * cosine + first_half * sine_part, source[..., rotary:]], axis=-1)

def layer(rows_in, weights, segment, cos_heads, sin_heads):
    gain_one, shift_one, qkv_weight, qkv_bias, out_weight, gain_two, shift_two, gate_weight, up_weight, down_weight = weights
    tokens = rows_in.shape[0]
    h_one = low(normalize(rows_in, gain_one, shift_one))
    linear = matmul(h_one, qkv_weight.reshape(D, 3 * D)).reshape(tokens, 3, H, HD) + qkv_bias[None]
    linear = low_back(linear)
    queries = low(low_back(turn(linear[:, 0], cos_heads, sin_heads, ROT)))
    key_rows = low(low_back(turn(linear[:, 1], cos_heads, sin_heads, ROT)))
    values = low(linear[:, 2])
    place = jnp.arange(tokens, dtype=jnp.int32)
    allowed = (place[None, :] <= place[:, None]) & (segment[:, None] == segment[None, :])
    factor = HD ** (-0.5)

    def one_head(operands):
        q_head, k_head, v_head = operands
        scores = low_back(matmul(q_head, k_head.T) * factor)
        scores = jnp.where(allowed, scores, masked_value)
        row_max = lax.optimization_barrier(jnp.max(scores, axis=-1, keepdims=True))
        exponent = jnp.exp(scores - row_max)
        probability = exponent / lax.optimization_barrier(jnp.sum(exponent, axis=-1, keepdims=True))
        return matmul(low(probability), v_head)
    attended = lax.map(jax.checkpoint(one_head), (queries.transpose(1, 0, 2), key_rows.transpose(1, 0, 2), values.transpose(1, 0, 2)))
    attended = low(low_back(attended.transpose(1, 0, 2).reshape(tokens, D)))
    branch = low_back(matmul(attended, out_weight.T))
    resid = rows_in + branch
    h_two = low(normalize(resid, gain_two, shift_two))
    gate_act = low_back(matmul(h_two, gate_weight))
    up_act = low_back(matmul(h_two, up_weight))
    hidden = low(jax.nn.silu(gate_act) * up_act)
    return resid + matmul(hidden, down_weight.T)

def reference(block_in, segments, positions, gain_one, shift_one, qkv_weight, qkv_bias, out_weight, gain_two, shift_two, gate_weight, up_weight, down_weight, grad_out):
    params = (gain_one.astype(jnp.float32), shift_one.astype(jnp.float32), qkv_weight.astype(jnp.float32), qkv_bias.astype(jnp.float32), out_weight.astype(jnp.float32), gain_two.astype(jnp.float32), shift_two.astype(jnp.float32), gate_weight.astype(jnp.float32), up_weight.astype(jnp.float32), down_weight.astype(jnp.float32))

    def one_sequence(carry, item):
        rows_in, segment, position, cotangent = item
        cosine, sine_part = rotation(position, ROT)
        cos_heads = cosine[:, None, :]
        sin_heads = sine_part[:, None, :]

        def forward(rows_f, weights):
            return layer(rows_f, weights, segment, cos_heads, sin_heads)
        out_rows, pullback = jax.vjp(forward, rows_in.astype(jnp.float32), params)
        d_rows, d_params = pullback(cotangent.astype(jnp.float32))
        carry = jax.tree.map(lambda left, right: left + right, carry, d_params)
        return (carry, (out_rows.astype(jnp.bfloat16), d_rows))
    start = jax.tree.map(jnp.zeros_like, params)
    totals, outputs = lax.scan(one_sequence, start, (block_in, segments, positions, grad_out))
    return (outputs[0], outputs[1], totals[0], totals[1], totals[2], totals[3], totals[4], totals[5], totals[6], totals[7], totals[8], totals[9])
```

```python
import heapq
import math

import jax
import jax.numpy as jnp
from jax import lax
from jax.experimental import pallas as pl
from jax.experimental.pallas import tpu as pltpu
from jax.sharding import PartitionSpec as P

ROT = 16
EPSILON = 1e-05
THETA = 10000.0
MASKED = -1e30
F32 = jnp.float32
BF16 = jnp.bfloat16
ANY = pl.BlockSpec(memory_space=pl.ANY)
VMEM = pl.BlockSpec(memory_space=pltpu.VMEM)
MESH = pl.DeviceIdType.MESH
LINK = 0.085e6
CHIP = 0.5e6
ROWS = 256
PLAN = {
    "forward_kernel": {
        (0, 1): 10.3, (1, 1): 10.9, (2, 1): 10.3, (4, 2): 57.0, (5, 3): 65.6, (6, 4): 140.0, (7, 4): 140.0,
        (8, 2): 14.5, (8, 3): 34.2, (8, 4): 54.4, (8, 5): 43.9, (9, 3): 31.0, (9, 4): 47.0, (9, 5): 66.1,
        (9, 6): 68.6, (10, 3): 35.5, (10, 4): 53.6, (10, 5): 78.9, (10, 6): 87.3, (11, 3): 74.9, (11, 4): 100.3,
        (11, 5): 111.3, (11, 6): 115.3, (12, 3): 93.8, (12, 4): 127.7, (12, 5): 167.3, (12, 6): 170.8, (13, 3): 176.4,
        (13, 4): 205.9, (13, 5): 227.9, (13, 6): 231.8, (14, 3): 185.1, (14, 4): 228.6, (14, 5): 248.6,
        (14, 6): 241.0, (15, 1): 4.8, (16, 2): 20.1, (16, 3): 28.2, (17, 2): 41.5, (17, 3): 78.0, (18, 1): 4.6,
        (18, 3): 10.5, (18, 5): 10.5, (20, 2): 45.8, (21, 2): 70.4, (22, 2): 89.1, (23, 2): 117.7, (24, 2): 103.7,
        (24, 3): 160.8, (25, 3): 173.0, (25, 5): 177.9, (25, 7): 182.6, (25, 9): 187.0, (25, 10): 190.8,
        (26, 31): 109.2, (27, 3): 163.5, (27, 4): 185.3, (28, 2): 195.6, (29, 2): 217.5, (29, 3): 230.7,
    },
    "feed_kernel": {
        (0, 3): 2.7, (0, 14): 78.4, (0, 16): 73.7, (1, 3): 39.6, (1, 4): 59.9, (2, 1): 89.7, (2, 2): 72.2,
        (3, 2): 107.6, (3, 3): 129.7, (4, 2): 51.9, (4, 3): 67.3, (4, 4): 85.0, (4, 5): 107.7, (4, 6): 113.7,
        (5, 2): 71.5, (5, 3): 89.0, (5, 4): 107.8, (5, 5): 113.6, (5, 6): 137.8,
    },
    "attend_back_kernel": {
        (0, 1): 0.2, (0, 2): 16.8, (0, 3): 42.3, (0, 4): 65.5, (0, 5): 79.3, (1, 2): 10.9, (1, 3): 30.6, (1, 4): 51.4,
        (1, 5): 79.0, (1, 6): 84.9, (2, 2): 18.0, (2, 3): 46.1, (2, 4): 73.6, (2, 5): 82.7, (2, 6): 97.0, (3, 1): 2.7,
        (3, 2): 47.3, (3, 3): 65.4, (4, 2): 30.7, (4, 3): 42.2, (5, 0): 2.7, (5, 22): 0.0, (5, 25): 78.2,
    },
    "last_kernel": {
        (0, 1): 2.7, (1, 1): 12.1, (2, 2): 25.8, (2, 3): 45.0, (3, 1): 2.7, (3, 2): 56.6, (4, 2): 58.4, (4, 3): 67.9,
        (4, 4): 64.3, (4, 5): 80.0, (5, 1): 4.4, (5, 2): 19.7, (5, 3): 51.1, (5, 4): 95.6, (5, 5): 105.8,
        (6, 2): 11.4, (6, 3): 26.5, (6, 4): 54.3, (6, 5): 85.5, (6, 6): 97.6, (7, 3): 23.7, (7, 4): 37.7,
        (7, 5): 79.2, (7, 6): 98.1, (7, 7): 110.3, (8, 3): 16.9, (8, 4): 53.1, (8, 5): 85.3, (8, 6): 100.1,
        (8, 7): 112.8, (9, 3): 31.2, (9, 4): 64.5, (9, 5): 97.7, (9, 6): 103.3, (9, 7): 114.8,
    },
}
GRAD_AFTER = 4
NEAR_LATE = 5
EARLY = (0, 0, 1, 0, 0, 0, 0)
SLACK = (0.0, 0.0, 0.0, 10.0, 10.0, 10.0, 5.0)


def mm(left, right):
    return jnp.dot(left, right, preferred_element_type=F32)


def mm_nt(left, right):
    return lax.dot_general(left, right, (((1,), (1,)), ((), ())), preferred_element_type=F32)


def mm_tn(left, right):
    return lax.dot_general(left, right, (((0,), (0,)), ((), ())), preferred_element_type=F32)


def shape(dims, dtype):
    return jax.ShapeDtypeStruct(tuple(dims), dtype)


def nbytes(ref):
    return math.prod(ref.shape) * jnp.dtype(ref.dtype).itemsize


class Event:
    def __init__(self):
        self.done = False
        self.waiters = []


class Copy:
    def __init__(self, kern, src, dst, to, into):
        self.kern = kern
        self.send_sem = kern.sem()
        self.recv_sem = kern.sem()
        self.desc = pltpu.make_async_remote_copy(src, dst, self.send_sem, self.recv_sem, device_id=to, device_id_type=MESH)
        into = dst if into is None else into
        self.arrival = pltpu.make_async_remote_copy(
            into, into, self.send_sem, self.recv_sem, device_id=to, device_id_type=MESH
        )

    def start(self, cond=None, late=True):
        self.cond = cond
        run_if(cond, self.desc.start)
        if late:
            self.kern.sent.append((cond, self.desc.wait_send))

    def gone(self):
        run_if(self.cond, self.desc.wait_send)

    def wait(self, cond=None):
        run_if(cond, self.arrival.wait_recv)


def run_if(cond, step):
    if cond is None:
        step()
    else:
        pl.when(cond)(lambda: step())


class Kern:
    def __init__(self, line, sems, name):
        self.line = line
        self.sems = sems
        self.used = 0
        self.sent = []
        self.now = 0.0
        self.queue = []
        self.count = 0
        self.busy = {}
        self.ended = []
        self.plan = PLAN.get(name, {}) if line == 4 else {}
        fsdp = lax.axis_index("fsdp")
        self.z = fsdp // 2
        self.x = lax.rem(fsdp, 2)
        self.y = lax.axis_index("ctx")
        self.c = lax.axis_index("tp")
        self.home = self.c == self.x
        self.away = self.c != self.x
        self.q = self.x * 2 + self.y
        self.nx = (self.z * 2 + 1 - self.x, self.y, self.c)
        self.ny = (fsdp, 1 - self.y, self.c)
        self.diag = (self.z * 2 + 1 - self.x, 1 - self.y, self.c)
        self.sib = (fsdp, self.y, 1 - self.c)
        self.has_up = self.z < line - 1
        self.has_dn = self.z > 0
        self.up = self.at_line(1)
        self.dn = self.at_line(-1)

    def segment(self, name, step):
        pass

    def sem(self):
        self.used += 1
        return self.sems.at[self.used - 1]

    def at_line(self, shift):
        n = self.line
        return (lax.rem(self.z + shift + n, n) * 2 + self.x, self.y, self.c)

    def greet(self):
        barrier = pltpu.get_barrier_semaphore()
        peers = 3 + self.line
        for to in (self.nx, self.ny, self.diag, self.sib):
            pl.semaphore_signal(barrier, inc=1, device_id=to, device_id_type=MESH)
        for d in range(1, self.line):
            pl.semaphore_signal(barrier, inc=1, device_id=self.at_line(d), device_id_type=MESH)
        pl.semaphore_wait(barrier, peers)

    def remote(self, src, dst, to, into=None):
        return Copy(self, src, dst, to, into)

    def local(self, src, dst):
        return pltpu.make_async_copy(src, dst, self.sem())

    def link(self, name, size, rate):
        end = max(self.now, self.busy.get(name, 0.0)) + size / rate
        self.busy[name] = end
        return end + 1.0

    def add(self, task, at=0.0):
        self.count += 1
        heapq.heappush(self.queue, (at, self.count, task))

    def fire(self, event):
        event.done = True
        for task in event.waiters:
            self.add(task, self.now)

    def run(self):
        steps = {}
        while self.queue:
            at, _, task = heapq.heappop(self.queue)
            self.now = max(self.now, at)
            while True:
                name, step = steps.setdefault(id(task), (len(steps), 0))
                steps[id(task)] = (name, step + 1)
                self.segment(name, step)
                try:
                    want = next(task)
                except StopIteration:
                    self.ended.append(task)
                    break
                if not isinstance(want, Event):
                    want = self.plan.get((name, step + 1), want)
                if isinstance(want, Event):
                    if want.done:
                        continue
                    want.waiters.append(task)
                    break
                self.add(task, want)
                break
        for cond, wait in self.sent:
            run_if(cond, wait)


def call(body, ins, outs, scratch, line, cid, sems, vmem_mb, name, flops=0):
    def run(*refs):
        kern = Kern(line, refs[-1], name)
        kern.greet()
        body(kern, refs[: len(ins)], refs[len(ins) : len(ins) + len(outs)], refs[len(ins) + len(outs) : -1])
        kern.run()
        assert kern.used <= sems, kern.used

    return pl.pallas_call(
        run,
        out_shape=[out for out, _ in outs],
        in_specs=[spec for _, spec in ins],
        out_specs=[spec for _, spec in outs],
        scratch_shapes=list(scratch) + [pltpu.SemaphoreType.DMA((sems,))],
        compiler_params=pltpu.CompilerParams(
            collective_id=cid, has_side_effects=True, vmem_limit_bytes=vmem_mb * 1024 * 1024
        ),
        name=name,
    )(*[array for array, _ in ins])


def rows_loop(total, step, body):
    @pl.loop(0, total // step)
    def _(index):
        body(pl.ds(pl.multiple_of(index * step, step), step))


def store_rows(target, lead, i, value, rows):
    chunk, cols = value.shape
    count = chunk // rows
    if count <= 4:
        share = 4 // count
        target[lead + (i // share, pl.ds(lax.rem(i, share) * count, count))] = value.reshape(count, rows, cols)
    else:
        target[lead + (pl.ds(i * (count // 4), count // 4),)] = value.reshape(count // 4, 4, rows, cols)


def plane_gather(k, own, full, ready=None, sent=None, done=None, slack=0.0):
    if ready is not None:
        yield ready
    tokens = own.shape[0]
    size = nbytes(own) / 2
    a, b = pl.ds(0, tokens // 2), pl.ds(tokens // 2, tokens // 2)
    y, o = k.y, 1 - k.y
    keep = k.local(own, full.at[y])
    x_a = k.remote(own.at[a], full.at[y, a], k.nx)
    y_b = k.remote(own.at[b], full.at[y, b], k.ny, into=full.at[o, b])
    x_b = k.remote(own.at[b], full.at[y, b], k.nx)
    y_a = k.remote(own.at[a], full.at[y, a], k.ny, into=full.at[o, a])
    pass_y = k.remote(full.at[y, a], full.at[y, a], k.ny, into=full.at[o, a])
    pass_x = k.remote(full.at[o, b], full.at[o, b], k.nx)
    for copy in (x_a, y_b, x_b, y_a):
        copy.start(k.home)
    pl.when(k.home)(keep.start)
    k.link("x", size, LINK)
    yield k.link("y", size, LINK) + slack
    x_a.wait(k.away)
    pass_y.start(k.away)
    y_b.wait(k.home)
    pass_x.start(k.home)
    if sent is not None:
        k.fire(sent)
    k.link("x", 2 * size, LINK)
    yield k.link("y", 2 * size, LINK) + slack
    x_b.wait(k.away)
    y_a.wait(k.home)
    pass_y.wait(k.away)
    pass_x.wait(k.away)
    pl.when(k.home)(keep.wait)
    if done is not None:
        k.fire(done)


def plane_scatter(k, part, got, sx, sy, far=None, ready=None, done=None):
    if far is not None:
        yield far
    half = part.shape[1] // 2
    size = nbytes(part) / 4
    a, b = pl.ds(0, half), pl.ds(half, half)
    y, o = k.y, 1 - k.y
    y_far = k.remote(part.at[o, a], got, k.ny)
    x_far = k.remote(part.at[o, b], got, k.nx)
    y_a = k.remote(part.at[o, a], sy.at[a], k.ny)
    x_b = k.remote(part.at[y, b], sx.at[b], k.nx)
    x_a = k.remote(part.at[y, a], sx.at[a], k.nx)
    y_b = k.remote(part.at[o, b], sy.at[b], k.ny)
    y_far.start(k.away)
    x_far.start(k.away)
    y_a.start(k.home)
    k.link("x", 2 * size, LINK)
    when = k.link("y", 2 * size, LINK)
    if ready is not None:
        yield ready
    x_b.start(k.away)
    yield when
    y_far.wait(k.away)
    x_far.wait(k.home)
    index = jnp.where(k.home, o, y)
    first = jnp.where(k.home, half, 0)

    @pl.loop(0, half // 32)
    def _(i):
        at = pl.ds(pl.multiple_of(first + i * 32, 32), 32)
        more = got[pl.ds(pl.multiple_of(i * 32, 32), 32), :]
        part[index, at, :] = (part[index, at, :].astype(F32) + more.astype(F32)).astype(BF16)

    k.now += 1.0
    x_a.start(k.away)
    y_b.start(k.home)
    k.link("x", size, LINK)
    yield k.link("y", size, LINK)
    x_b.wait(k.home)
    x_a.wait(k.home)
    y_a.wait(k.home)
    y_b.wait(k.home)
    if done is not None:
        k.fire(done)


def scatter_scratch(tokens, width):
    return [
        pltpu.VMEM((tokens // 2, width), BF16),
        pltpu.VMEM((tokens, width), BF16),
        pltpu.VMEM((tokens, width), BF16),
    ]


def scatter_sum(k, part, sx, sy, at):
    return part[k.y, at, :].astype(F32) + sx[at, :].astype(F32) + sy[at, :].astype(F32)


def near_gather(k, source, block, event):
    own = source(k.q)
    near = k.remote(source((1 - k.x) * 2 + k.y), block(0, k.z, k.x), k.nx, into=block(0, k.z, 1 - k.x))
    keep = k.local(own, block(0, k.z, k.x))
    near.start()
    keep.start()
    yield k.link("x", nbytes(own) * 2, LINK)
    near.wait()
    keep.wait()
    k.fire(event)


def line_gather(k, pair, size, ready=(), early=0, following=None, done=None, slack=0.0, first=None):
    n = k.line
    z = k.z

    def at_line(shift):
        return lax.rem(z + shift + n, n)

    def send(src, spot, arrival, to, ok):
        copy = k.remote(src, spot, to, into=arrival)
        copy.start(ok)
        return copy

    heads = []
    if first is not None and n > 1:
        own, block = first
        heads.append(
            (
                send(own, block(0, z, k.x), block(0, at_line(-1), k.x), k.up, k.has_up),
                send(own, block(0, z, k.x), block(0, at_line(1), k.x), k.dn, k.has_dn),
            )
        )
    for event in ready:
        yield event

    hop = size / LINK
    end = k.link("z", size * (n - 1), LINK) if n > 1 else k.now + 1.0
    across = []
    moving = None
    for d in range(n):
        if d:
            yield max(k.now, end - (n - 1 - d) * hop) + slack
        up_ok, dn_ok = z >= d, z + d < n
        left, right = at_line(-d), at_line(d)
        if d:
            for up, dn in moving:
                up.wait(up_ok)
                dn.wait(dn_ok)
        if d == 0 and heads:
            near = first[1](0, z, 1 - k.x)
            heads.append(
                (
                    send(near, near, first[1](0, at_line(-1), 1 - k.x), k.up, k.has_up),
                    send(near, near, first[1](0, at_line(1), 1 - k.x), k.dn, k.has_dn),
                )
            )
            moving = heads
        elif d < n - 1:
            up = send(pair(0, left), pair(0, left), pair(0, at_line(-d - 1)), k.up, up_ok & k.has_up)
            dn = send(pair(0, right), pair(0, right), pair(0, at_line(d + 1)), k.dn, dn_ok & k.has_dn)
            moving = [(up, dn)]
        if d == min(early, n - 1) and following is not None:
            k.fire(following)
        for index, ok in ((left, up_ok), (right, dn_ok)) if d else ((z, None),):
            copy = k.remote(pair(0, index), pair(1, index), k.sib)
            copy.start(ok)
            across.append((copy, ok))
    yield k.now + size / 2 / CHIP + 1.0
    for copy, ok in across:
        copy.wait(ok)
    if done is not None:
        k.fire(done)


def line_scatter(
    k, own, sib_part, sibling, from_dn, from_up, got, rows=None, own_part=None, ready=(), following=None, done=None, early=0, slack=0.0
):
    for event in ready:
        yield event
    n = k.line
    z = k.z
    first, count = rows or (0, own.shape[2])
    part = pl.ds(first, count)
    size = nbytes(own) * 2 / n * count / own.shape[2]
    hop = size / LINK
    step = min(count, 64)
    spot = [lax.rem(z + d, n) for d in range(n)]
    order = []
    for d in range(n - 1, 0, -1):
        for e in (d, n - d):
            if e not in order:
                order.append(e)
    order.append(0)
    loads, crosses = {}, {}
    for d in order:
        if own_part is not None:
            loads[d] = k.local(own_part.at[spot[d], :, part], own.at[spot[d], :, part])
            loads[d].start()
        crosses[d] = k.remote(sib_part.at[spot[d], :, part], sibling.at[spot[d], :, part], k.sib)
        crosses[d].start()

    def plus(index, source):
        for quarter in range(4):

            def add(at):
                at = pl.ds(pl.multiple_of(first + at.start, 16), at.size)
                more = source(quarter, at)
                own[index, quarter, at, :] = (own[index, quarter, at, :].astype(F32) + more.astype(F32)).astype(BF16)

            rows_loop(count, step, add)

    def prepare(d):
        if d in loads:
            loads[d].wait()
        crosses[d].wait()
        plus(spot[d], lambda quarter, at: sibling[spot[d], quarter, at, :])
        k.now += size / 2.0e6

    def take(d, source, index, cond):
        pl.when(cond)(lambda: plus(index, lambda quarter, at: source[d, quarter, at, :]))
        k.now += size / 2.0e6

    yield k.link("c", size * n / 2, CHIP)
    up = down = None
    end = k.link("z", size * (n - 1), LINK) if n > 1 else k.now
    for d in range(n - 1, -1, -1):
        for e in (d, n - d):
            if e in order:
                prepare(e)
                order.remove(e)
        up_ok, dn_ok = (z >= 1) & (z + d < n), (z <= n - 2) & (z >= d)
        if d < n - 1:
            up.wait(up_ok)
            take(d, from_dn, spot[d], up_ok)
        if d:
            after = k.remote(own.at[spot[d], :, part], from_dn.at[d - 1, :, part], k.up)
            if up is not None:
                up.gone()
            after.start((z + d < n) & k.has_up, late=False)
            up = after
        if d < n - 1:
            down.wait(dn_ok)
            take(d, from_up, spot[(n - d) % n], dn_ok)
        if d:
            after = k.remote(own.at[spot[n - d], :, part], from_up.at[d - 1, :, part], k.dn)
            if down is not None:
                down.gone()
            after.start((z >= d) & k.has_dn, late=False)
            down = after
        if d == n - 1 - early and following is not None:
            k.fire(following)
        if d:
            yield max(k.now, end - (d - 1) * hop) + slack
    for copy in (up, down):
        if copy is not None:
            copy.gone()
    yield from quarters_exchange(k, own.at[z, :, part], got.at[:, part])
    if done is not None:
        k.fire(done)


def quarters_exchange(k, block, got):
    keep = k.local(block.at[k.q], got.at[k.q])
    keep.start()
    copies = []
    for away, to in ((3, k.diag), (2, k.nx), (1, k.ny)):
        other = (1 - k.x if away & 2 else k.x) * 2 + (1 - k.y if away & 1 else k.y)
        copy = k.remote(block.at[other], got.at[k.q], to, into=got.at[other])
        copy.start()
        copies.append(copy)
    size = nbytes(got) / 2
    k.link("x", size, LINK)
    yield k.link("y", size, LINK)
    for copy in copies:
        copy.wait()
    keep.wait()


def line_scratch(line, rows, cols):
    more = max(line - 1, 1)
    return [pltpu.VMEM((line, 4, rows, cols), BF16)] + [pltpu.VMEM((more, 4, rows, cols), BF16) for _ in range(2)]


def line_sems(line):
    return 14 * line + 20


def norm_rows(source):
    average = jnp.mean(source, axis=-1, keepdims=True)
    centered = source - average
    inv_std = lax.rsqrt(jnp.mean(centered * centered, axis=-1, keepdims=True) + EPSILON)
    return centered * inv_std, inv_std


def norm_back(gradient, scaled, inv_std, gain_vec):
    inner = gradient * gain_vec
    return inv_std * (
        inner - jnp.mean(inner, axis=-1, keepdims=True) - scaled * jnp.mean(inner * scaled, axis=-1, keepdims=True)
    )


def fold(rows):
    return rows[:8] + rows[8:]


def head_mask(rows, side, dtype):
    lane = lax.broadcasted_iota(jnp.int32, (rows, 128), 1)
    return (lane // 64 == side).astype(dtype)


def turn_lanes(value, cosine, sine_a, sine_b):
    return value * cosine + pltpu.roll(value, 120, 1) * sine_a + pltpu.roll(value, 8, 1) * sine_b


def expand_tables(tables, cosine, sine_a, sine_b):
    tokens = tables.shape[1]
    lane = lax.broadcasted_iota(jnp.int32, (128, 128), 1)
    spot = lax.rem(lane, 64)
    for half in range(2):

        def step(at):
            value = tables[half, at, :]
            other = pltpu.roll(value, 64, 1)
            sine = jnp.where(lane < 64, other, value)
            full = pl.ds(pl.multiple_of(half * tokens + at.start, 128), 128)
            cosine[full, :] = jnp.where(spot < 16, jnp.where(lane < 64, value, other), 1.0)
            sine_a[full, :] = jnp.where(spot < 8, -sine, 0.0)
            sine_b[full, :] = jnp.where((spot >= 8) & (spot < 16), sine, 0.0)

        rows_loop(tokens, 128, step)


def mark_documents(tables, key_marks, query_marks):
    tokens = tables.shape[1]
    lane = lax.broadcasted_iota(jnp.int32, (128, 128), 1)
    for half in range(2):

        def step(at):
            segment = tables[half, at, 32:33].astype(jnp.int32)
            full = pl.ds(pl.multiple_of(half * tokens + at.start, 128), 128)
            for side in range(2):
                document = lane - (1 - side) * 64
                same = document == segment
                used = (document >= 0) & (document < 4)
                key_marks[side, full, :] = jnp.where(same, 1.0, 0.0).astype(BF16)
                query_marks[side, full, :] = jnp.where(used & jnp.logical_not(same), MASKED, 0.0).astype(BF16)

        rows_loop(tokens, 128, step)


BLOCK = 256


def causal(scores):
    key = lax.broadcasted_iota(jnp.int32, scores.shape, 0)
    query = lax.broadcasted_iota(jnp.int32, scores.shape, 1)
    return jnp.where(key <= query, scores, MASKED)


def mark_keys(k_ref, pair, key_marks, marked):
    length = k_ref.shape[1]
    for side in range(2):
        marked[side] = k_ref[pair] * head_mask(length, side, BF16) + key_marks[side]


def attention_forward(k, q_ref, v_ref, marked, query_marks, out_ref, out_t, lse_ref, pair, out_lanes):
    length = q_ref.shape[1]
    v_t = v_ref[pair].astype(F32).T.astype(BF16)
    for i in range(length // BLOCK):
        low, extent = i * BLOCK, (i + 1) * BLOCK
        at = slice(low, extent)
        sides = []
        for side in range(2):
            queries = q_ref[pair, at, :] * head_mask(BLOCK, side, BF16) + query_marks[side, at, :]
            scores = [causal(mm_nt(marked[side, at, :], queries))]
            if i:
                scores.append(mm_nt(marked[side, :low, :], queries))
            tops = [jnp.max(part, axis=0, keepdims=True) for part in scores]
            top = jnp.maximum(tops[0], tops[1]) if i else tops[0]
            weights = [jnp.exp(part - top) for part in scores]
            total = sum(jnp.sum(part, axis=0, keepdims=True) for part in weights)
            rows = slice(side * 64, side * 64 + 64)
            value = mm(v_t[rows, at], weights[0].astype(BF16))
            if i:
                value = value + mm(v_t[rows, :low], weights[1].astype(BF16))
            sides.append(value * (1.0 / total))
            lse_ref[pair, side : side + 1, at] = top + jnp.log(total)
        both = jnp.concatenate(sides, axis=0)
        out_t[pair, :, at] = both
        out_ref[at, out_lanes] = both.T.astype(BF16)
        k.now += 0.5 + 0.3 * i
        yield k.now


def attention_backward(k, q_ref, v_ref, marked, query_marks, out_t, lse_ref, do_ref, dq_t, dk, dv, k_ref, pair):
    length = q_ref.shape[1]
    k_t = k_ref[pair].astype(F32).T.astype(BF16)
    inner = do_ref[pair].astype(F32).T * out_t[pair]
    inner = [jnp.sum(inner[side * 64 : side * 64 + 64], axis=0, keepdims=True) for side in range(2)]
    for i in range(length // BLOCK):
        at = slice(i * BLOCK, (i + 1) * BLOCK)
        for side in range(2):
            mask = head_mask(BLOCK, side, BF16)
            plain = q_ref[pair, at, :] * mask
            queries = plain + query_marks[side, at, :]
            grads = do_ref[pair, at, :] * mask
            lse = lse_ref[pair, side : side + 1, at]
            turned = None
            for j in range(i, -1, -1):
                of = slice(j * BLOCK, (j + 1) * BLOCK)
                scores = mm_nt(marked[side, of, :], queries)
                if j == i:
                    scores = causal(scores)
                probability = jnp.exp(scores - lse)
                d_prob = mm_nt(v_ref[pair, of, :], grads)
                d_scores = (probability * (d_prob - inner[side][:, at])).astype(BF16)
                part_v = mm(probability.astype(BF16), grads)
                part_k = mm(d_scores, plain)
                if j == i and side == 0:
                    dv[of, :] = part_v
                    dk[of, :] = part_k
                else:
                    dv[of, :] += part_v
                    dk[of, :] += part_k
                part_q = mm(k_t[side * 64 : side * 64 + 64, of], d_scores)
                turned = part_q if turned is None else turned + part_q
            dq_t[side * 64 : side * 64 + 64, at] = turned
        k.now += 1.0 + 0.8 * i
        yield k.now


def forward_kernel(line, x, gains, grad, table, bias, qkv, out_w, gate, up, down):
    tokens, width = x.shape
    length = 2 * tokens
    rows = width // (2 * line)
    cols_q = out_w.shape[1] // 4
    ff = gate.shape[1]
    ff_q = ff // 4
    pairs = cols_q // 64

    def body(k, ins, outs, scratch):
        x, gains, grad, table, bias, qkv, out_w, gate, up, down = ins
        h_out, g_out, h2_out, resid, w_qkv, w_out, w_gate, w_up, w_down = outs[:9]
        q_out, key_out, v_out, o_out, o_t_out, lse, tables, d_hid_out = outs[9:]
        h_own, h_full, b_full, wq, wo, whole, pieces, cosine, sine_a, sine_b, key_marks, query_marks, marked, part, got, sx, sy, r_own, h2_own = scratch[:-8]
        q, key, v, o, o_t, g_full, w_d, d_hid = scratch[-8:]
        h_there, t_there, b_there, g_there = (Event() for _ in range(4))
        loaded_out, far, parted, summed, h2_ready = (Event() for _ in range(5))
        loaded_qkv = [Event() for _ in range(3)]
        cut = [Event() for _ in range(3)]
        h_sent, g_sent = Event(), Event()

        def norm_one():
            @pl.when(k.home)
            def _():
                def step(at):
                    scaled, _ = norm_rows(x[at, :].astype(F32))
                    h_own[at, :] = (scaled * gains[0:1, :] + gains[1:2, :]).astype(BF16)

                rows_loop(tokens, 16, step)

            k.now += 3.0
            yield k.now

        def share_bias():
            copy = k.remote(bias, b_full.at[1], k.sib)
            copy.start()
            b_full[0] = bias[...]
            yield k.now + 3.0
            copy.wait()
            k.fire(b_there)

        def cut_quarters():
            weight = whole
            for i in (2, 0, 1):
                load = k.local((gate, up, down)[i], whole)
                load.start()
                yield k.now + 1.5
                load.wait()
                for quarter in range(4):
                    low = quarter * ff_q
                    base = low // 128 * 128
                    top = min(-(-(low + ff_q) // 128) * 128, ff)

                    for half in range(2):

                        def step(at):
                            full = pl.ds(pl.multiple_of(half * (rows // 2) + at.start, 16), 16)
                            value = weight[full, base:top].astype(F32)
                            if low != base:
                                value = pltpu.roll(value, value.shape[1] - (low - base), 1)
                            pieces[i, quarter, half, at, :] = value[:, :ff_q].astype(BF16)

                        rows_loop(rows // 2, 16, step)
                k.now += 1.5
                k.fire(cut[i])
                yield k.now

        def prepare():
            yield t_there
            expand_tables(tables, cosine, sine_a, sine_b)
            mark_documents(tables, key_marks, query_marks)
            k.now += 2.0
            yield k.now

        def fetch(source, target, event, ready):
            yield event
            copy = k.local(source, target)
            copy.start()
            yield k.now + nbytes(target) / 3.0e6 + 1.0
            copy.wait()
            k.fire(ready)

        def work():
            yield h_there
            store = k.local(h_full, h_out)
            store.start()
            yield b_there

            def project(j, slot, half, at):
                full = pl.ds(pl.multiple_of(half * tokens + at.start, 256), at.size)
                value = mm(h_full[half, at, :], wq[slot, j].reshape(width, cols_q)) + b_full[slot, j : j + 1, :]
                for pp in range(cols_q // 128):
                    piece = value[:, pp * 128 : pp * 128 + 128]
                    if j < 2:
                        piece = turn_lanes(piece, cosine[full, :], sine_a[full, :], sine_b[full, :])
                    if j == 0:
                        piece = piece * 0.125
                    (q, key, v)[j][slot * 2 + pp, full, :] = piece.astype(BF16)

            for j in range(3):
                yield loaded_qkv[j]
                for slot in range(2):
                    for half in range(2):
                        rows_loop(tokens, 512, lambda at: project(j, slot, half, at))
                    k.now += 1.5
                    yield k.now
            for slot in range(2):
                for pp in range(cols_q // 128):
                    pair = slot * 2 + pp
                    mark_keys(key, pair, key_marks, marked)
                    lanes = slice(pp * 128, pp * 128 + 128)
                    yield from attention_forward(k, q, v, marked, query_marks, o.at[slot], o_t, lse, pair, lanes)
            stores = [store] + [
                k.local(source, target)
                for source, target in ((q, q_out), (key, key_out), (v, v_out), (o, o_out), (o_t, o_t_out))
            ]
            for copy in stores[1:]:
                copy.start()
            yield loaded_out
            for half, event in ((1 - k.y, far), (k.y, parted)):

                def close(at):
                    full = pl.ds(pl.multiple_of(half * tokens + at.start, 256), at.size)
                    value = sum(mm_nt(o[slot, full, :], wo[slot].reshape(width, cols_q)) for slot in range(2))
                    part[half, at, :] = value.astype(BF16)

                rows_loop(tokens, 512, close)
                k.now += 2.0
                k.fire(event)
                yield k.now
            yield k.now + 5.0
            for copy in stores:
                copy.wait()

        def hidden_back():
            yield g_there
            yield streamed[4]
            stores = []
            for side in range(2):
                load = k.local(w_down.at[side], w_d)
                load.start()
                for half in range(2):
                    fetch = k.local(g_out.at[half], g_full)
                    fetch.start()
                    yield k.now + 2.0
                    if half == 0:
                        load.wait()
                    fetch.wait()
                    if len(stores) >= 2:
                        stores[-2].wait()
                    d_hid[half] = mm(g_full[...], w_d[...].reshape(width, ff_q)).astype(BF16)
                    k.now += 2.5
                    stores.append(k.local(d_hid.at[half], d_hid_out.at[side, half]))
                    stores[-1].start()
                    yield k.now
            for store in stores[-2:]:
                store.wait()

        def norm_two():
            yield summed

            @pl.when(k.home)
            def _():
                def step(at):
                    value = x[at, :].astype(F32) + scatter_sum(k, part, sx, sy, at)
                    r_own[at, :] = value
                    scaled, _ = norm_rows(value)
                    h2_own[at, :] = (scaled * gains[2:3, :] + gains[3:4, :]).astype(BF16)

                rows_loop(tokens, 16, step)

            k.now += 4.0
            k.fire(h2_ready)
            keep = k.local(r_own, resid)
            pl.when(k.home)(keep.start)
            yield k.now + 20.0
            pl.when(k.home)(keep.wait)

        def columns(q):
            return pl.ds(pl.multiple_of(q * cols_q, cols_q), cols_q)

        units = []
        for j in range(3):
            units.append(
                (
                    lambda q, j=j: qkv.at[j, :, columns(q)],
                    lambda slot, z, x, j=j: w_qkv.at[slot, j, z, x],
                    lambda slot, z, j=j: w_qkv.at[slot, j, z],
                )
            )
        units.append(
            (lambda q: out_w.at[:, columns(q)], lambda slot, z, x: w_out.at[slot, z, x], lambda slot, z: w_out.at[slot, z])
        )
        for i, target in ((2, w_down), (0, w_gate), (1, w_up)):
            units.append(
                (
                    lambda q, i=i: pieces.at[i, q],
                    lambda slot, z, x, target=target: target.at[slot, z, pl.ds(2 * x, 2)],
                    lambda slot, z, target=target: target.at[slot, z],
                )
            )
        nears = [Event() for _ in units]
        going = [Event() for _ in units]
        streamed = [Event() for _ in units]

        def near_of(i):
            if i >= 3:
                yield h_sent
            if i >= NEAR_LATE:
                yield g_sent
            if i >= 4:
                yield cut[(2, 0, 1)[i - 4]]
            yield from near_gather(k, units[i][0], units[i][1], nears[i])

        for i in range(3):
            k.add(near_of(i))
        k.add(norm_one())
        for i in range(3, len(units)):
            k.add(near_of(i))
        for i, (source, block, pair) in enumerate(units):
            ready = (nears[i],) + ((going[i - 1],) if i else ())
            k.add(
                line_gather(
                    k,
                    pair,
                    nbytes(source(0)) * 4,
                    ready=ready,
                    early=EARLY[i],
                    following=going[i],
                    done=streamed[i],
                    slack=SLACK[i],
                    first=(source(k.q), block) if i < 3 else None,
                )
            )
        k.add(share_bias())
        k.add(plane_gather(k, table, tables, ready=nears[2], done=t_there))
        k.add(plane_gather(k, h_own, h_full, ready=nears[2], sent=h_sent, done=h_there))
        k.add(cut_quarters())
        k.add(prepare())
        for j in range(3):
            k.add(fetch(w_qkv.at[:, j], wq.at[:, j], streamed[j], loaded_qkv[j]))
        k.add(fetch(w_out, wo, streamed[3], loaded_out))
        k.add(plane_gather(k, grad, g_out, ready=nears[GRAD_AFTER], sent=g_sent, slack=15.0, done=g_there))
        k.add(hidden_back())
        k.add(work())
        k.add(plane_scatter(k, part, got, sx, sy, far=far, ready=parted, done=summed))
        k.add(norm_two())
        k.add(plane_gather(k, h2_own, h2_out, ready=h2_ready))

    ff_shape = (shape((2, line, 4, rows // 2, ff_q), BF16), ANY)
    plane = (shape((2, tokens, width), BF16), ANY)
    heads = (shape((2 * pairs // 2, length, 128), BF16), ANY)
    return call(
        body,
        [(x, VMEM), (gains, VMEM), (grad, ANY), (table, ANY), (bias, VMEM), (qkv, ANY), (out_w, ANY)]
        + [(gate, ANY), (up, ANY), (down, ANY)],
        [
            plane,
            plane,
            plane,
            (shape((tokens, width), F32), ANY),
            (shape((2, 3, line, 2, rows, cols_q), BF16), ANY),
            (shape((2, line, 2, rows, cols_q), BF16), ANY),
            ff_shape,
            ff_shape,
            ff_shape,
            heads,
            heads,
            heads,
            (shape((2, length, cols_q), BF16), ANY),
            (shape((2 * pairs // 2, 128, length), F32), ANY),
            (shape((2 * pairs // 2, 8, length), F32), VMEM),
            (shape((2, tokens, 128), F32), VMEM),
            (shape((2, 2, tokens, ff_q), BF16), ANY),
        ],
        [
            pltpu.VMEM((tokens, width), BF16),
            pltpu.VMEM((2, tokens, width), BF16),
            pltpu.VMEM((2,) + bias.shape, F32),
            pltpu.VMEM((2, 3, line, 2, rows, cols_q), BF16),
            pltpu.VMEM((2, line, 2, rows, cols_q), BF16),
            pltpu.VMEM((rows, ff), BF16),
            pltpu.VMEM((3, 4, 2, rows // 2, ff_q), BF16),
            pltpu.VMEM((length, 128), F32),
            pltpu.VMEM((length, 128), F32),
            pltpu.VMEM((length, 128), F32),
            pltpu.VMEM((2, length, 128), BF16),
            pltpu.VMEM((2, length, 128), BF16),
            pltpu.VMEM((2, length, 128), BF16),
            pltpu.VMEM((2, tokens, width), BF16),
        ]
        + scatter_scratch(tokens, width)
        + [pltpu.VMEM((tokens, width), F32), pltpu.VMEM((tokens, width), BF16)]
        + [pltpu.VMEM((2 * pairs // 2, length, 128), BF16) for _ in range(3)]
        + [
            pltpu.VMEM((2, length, cols_q), BF16),
            pltpu.VMEM((2 * pairs // 2, 128, length), F32),
            pltpu.VMEM((tokens, width), BF16),
            pltpu.VMEM((line, 4, rows // 2, ff_q), BF16),
            pltpu.VMEM((2, tokens, ff_q), BF16),
        ],
        line,
        1,
        120 + 10 * line_sems(line),
        62,
        "forward_kernel",
    )


def feed_kernel(line, h2, grad_all, w_gate, w_up, w_down, d_hid, resid, grad, gain):
    _, tokens, width = h2.shape
    length = 2 * tokens
    rows, ff_q = w_gate.shape[3:]
    chunk = 512

    def body(k, ins, outs, scratch):
        h2_in, g_in, w_gate, w_up, w_down, d_hid_in, resid, grad, gain = ins
        mixed_out, dr_out, dr_full, vectors, low_own, low_sib, high_own, high_sib, up_own, up_sib, got_down = outs
        h2, g, w, hid, d_gate, d_up, part, got, sx, sy, r_own, drb_own = scratch[:12]
        buffers, d_hid, free_down = scratch[12:-2], scratch[-2], scratch[-1]
        far, parted, summed, dr_ready, down_there = (Event() for _ in range(5))
        loads = {}

        def load(name, source, target):
            copy = k.local(source, target)
            copy.start()
            loads[name] = copy

        def weight(slot):
            return w[slot].reshape(width, ff_q)

        def half_weight(slot, side):
            return w[slot, side * line // 2 : (side + 1) * line // 2].reshape(width // 2, ff_q)

        def work():
            load("h2", h2_in, h2)
            for side in range(2):
                load(("gate", side), w_gate.at[side], w.at[side])
                load(("up", side), w_up.at[side], w.at[2 + side])
                if side == 0:
                    load("d_hid", d_hid_in, d_hid)
            load("g", g_in, g)
            for side in range(2):
                load(("down", side), w_down.at[side], w.at[4 + side])
            yield k.now + 5.0
            for index, (half, event) in enumerate(((1 - k.y, far), (k.y, parted))):

                @pl.loop(0, tokens // ROWS)
                def _(i):
                    at = pl.ds(pl.multiple_of(i * ROWS, ROWS), ROWS)

                    def need(name):
                        if index == 0:
                            pl.when(i == 0)(loads[name].wait)

                    need("h2")
                    rows_h = h2[half, at, :]
                    for side in range(2):
                        need(("gate", side))
                        gate_act = mm(rows_h, weight(side))
                        need(("up", side))
                        up_act = mm(rows_h, weight(2 + side))
                        if side == 0:
                            need("d_hid")
                        d_hidden = d_hid[side, half, at, :].astype(F32)
                        sigmoid_g = 1.0 / (1.0 + jnp.exp(-gate_act))
                        silu = gate_act * sigmoid_g
                        hid[side, half, at, :] = (silu * up_act).astype(BF16)
                        d_gate[side, half, at, :] = (
                            d_hidden * up_act * sigmoid_g * (1.0 + gate_act * (1.0 - sigmoid_g))
                        ).astype(BF16)
                        d_up[side, half, at, :] = (d_hidden * silu).astype(BF16)
                    for cols in range(2):
                        value = sum(
                            mm_nt(d_gate[side, half, at, :], half_weight(side, cols))
                            + mm_nt(d_up[side, half, at, :], half_weight(2 + side, cols))
                            for side in range(2)
                        )
                        part[half, at, cols * width // 2 : (cols + 1) * width // 2] = value.astype(BF16)

                k.now += 14.0
                k.fire(event)
                yield k.now
            pl.semaphore_signal(free_down, inc=1, device_id=k.sib, device_id_type=MESH)
            pl.semaphore_wait(free_down, 1)
            for name in ("g", ("down", 0), ("down", 1)):
                loads[name].wait()
            for quart in range(4):
                outer(g, ((hid, 0, 0), (hid, 1, 1)), quart)
                k.now += 1.7
                yield k.now
            k.fire(down_there)
            for half in range(2):
                for i in range(tokens // 512):
                    at = pl.ds(i * 512, 512)
                    for cols in range(2):
                        value = sum(mm_nt(hid[side, half, at, :], half_weight(4 + side, cols)) for side in range(2))
                        g[half, at, cols * width // 2 : (cols + 1) * width // 2] = value.astype(BF16)
                    k.now += 3.0
                    yield k.now
            keep = k.local(g, mixed_out)
            keep.start()
            stores = []
            for quart in range(4):
                outer(h2, ((d_gate, 0, 3), (d_gate, 1, 4)), quart)
                k.now += 1.7
                yield k.now
            stores = []
            for slot, first, target in ((3, 0, low_own), (4, 0, low_sib), (3, 1, high_own), (4, 1, high_sib)):
                stores.append(k.local(w.at[slot, :, :, pl.ds(first * rows // 2, rows // 2)], target))
                stores[-1].start()
            up_stores = []
            for batch in range(2):
                for store in up_stores:
                    store.wait()
                up_stores = []

                @pl.loop(0, length // chunk)
                def _(i):
                    turned = turn_columns(h2, batch * (length // chunk) + i)
                    at = pl.ds(pl.multiple_of(lax.rem(i, tokens // chunk) * chunk, chunk), chunk)
                    for side in range(2):
                        value = mm(turned, d_up[side].reshape(length, ff_q))
                        hid[side, i // (tokens // chunk), at, :] = value.astype(BF16)

                for side, target in enumerate((up_own, up_sib)):
                    for piece in range(length // rows):
                        index = batch * (length // rows) + piece
                        low = piece * rows
                        source = hid.at[side, low // tokens, pl.ds(low % tokens, rows)]
                        up_stores.append(k.local(source, target.at[index // 4, index % 4]))
                        up_stores[-1].start()
                k.now += 3.5
                yield k.now
            yield k.now + 3.0
            for store in stores + up_stores + [keep]:
                store.wait()

        def turn_columns(left, i):
            columns = left[:, :, pl.ds(pl.multiple_of(i * chunk, chunk), chunk)].reshape(length, chunk)
            return columns.astype(F32).T.astype(BF16)

        def outer(left, items, quart):
            count = width // chunk // 4

            @pl.loop(quart * count, quart * count + count)
            def _(i):
                turned = turn_columns(left, i)
                for right, side, slot in items:
                    store_rows(w, (slot,), i, mm(turned, right[side].reshape(length, ff_q)).astype(BF16), rows)

        def back():
            count = tokens // 4
            loads = [k.local(resid.at[pl.ds(i * count, count)], r_own.at[i % 2]) for i in range(4)]
            stores = [k.local(r_own.at[i % 2], dr_out.at[pl.ds(i * count, count)]) for i in range(4)]
            fetch = k.local(grad, drb_own)
            for copy in (fetch, loads[0], loads[1]):
                pl.when(k.home)(copy.start)
            vectors[...] = jnp.zeros_like(vectors)
            yield summed

            @pl.when(k.home)
            def _():
                fetch.wait()
                for i in range(4):
                    loads[i].wait()

                    def step(at):
                        full = pl.ds(pl.multiple_of(i * count + at.start, 16), 16)
                        value = scatter_sum(k, part, sx, sy, full)
                        scaled, inv_std = norm_rows(r_own[i % 2, at, :])
                        d_resid = drb_own[full, :].astype(F32) + norm_back(value, scaled, inv_std, gain[...])
                        r_own[i % 2, at, :] = d_resid
                        drb_own[full, :] = d_resid.astype(BF16)
                        vectors[0:8, :] += fold(value * scaled)
                        vectors[8:16, :] += fold(value)

                    rows_loop(count, 16, step)
                    stores[i].start()
                    if i in (1, 2):
                        stores[i - 1].wait()
                        loads[i + 1].start()

            k.now += 7.0
            k.fire(dr_ready)
            yield k.now + 5.0
            for store in stores[2:]:
                pl.when(k.home)(store.wait)

        k.add(work())
        k.add(plane_scatter(k, part, got, sx, sy, far=far, ready=parted, done=summed))
        k.add(back())
        k.add(plane_gather(k, drb_own, dr_full, ready=dr_ready))
        lower, upper = (0, rows // 2), (rows // 2, rows // 2)
        going = [Event() for _ in range(2)]
        down = (w.at[0], w.at[1], w.at[2]) + tuple(buffers[:2]) + (got_down,)
        k.add(line_scatter(k, *down, rows=lower, ready=(down_there,), following=going[0]))
        k.add(line_scatter(k, *down, rows=upper, ready=(going[0],)))

    grads = (shape((line, 4, rows, ff_q), BF16), ANY)
    half_grads = (shape((line, 4, rows // 2, ff_q), BF16), ANY)
    return call(
        body,
        [(item, ANY) for item in (h2, grad_all, w_gate, w_up, w_down, d_hid, resid, grad)] + [(gain, VMEM)],
        [
            (shape((2, tokens, width), BF16), ANY),
            (shape((tokens, width), F32), ANY),
            (shape((2, tokens, width), BF16), ANY),
            (shape((16, width), F32), VMEM),
            half_grads,
            half_grads,
            half_grads,
            half_grads,
            grads,
            grads,
            (shape((4, rows, ff_q), BF16), ANY),
        ],
        [
            pltpu.VMEM((2, tokens, width), BF16),
            pltpu.VMEM((2, tokens, width), BF16),
            pltpu.VMEM((6, line, 4, rows, ff_q), BF16),
            pltpu.VMEM((2, 2, tokens, ff_q), BF16),
            pltpu.VMEM((2, 2, tokens, ff_q), BF16),
            pltpu.VMEM((2, 2, tokens, ff_q), BF16),
            pltpu.VMEM((2, tokens, width), BF16),
        ]
        + scatter_scratch(tokens, width)
        + [pltpu.VMEM((2, tokens // 4, width), F32), pltpu.VMEM((tokens, width), BF16)]
        + line_scratch(line, rows, ff_q)[1:]
        + [pltpu.VMEM((2, 2, tokens, ff_q), BF16), pltpu.SemaphoreType.REGULAR],
        line,
        2,
        80 + 16 * line + 3 * line_sems(line),
        63,
        "feed_kernel",
    )


def attend_back_kernel(line, dr, w_out, w_qkv, q, key, v, lse, o_t, tables, mixed, resid, gate, up):
    _, tokens, width = dr.shape
    length = 2 * tokens
    cols_q = w_out.shape[-1]
    rows, ff_q = up[0].shape[2:]

    def body(k, ins, outs, scratch):
        dr_in, w_out, w_qkv, q, key, v, lse, o_t, tables, mixed, resid, gate_own, gate_sib, up_own, up_sib = ins
        dlin, bias, part_h, block_out, got_gate, got_up = outs
        wq, do, dq_t, dk, dv, cosine, sine_a, sine_b, key_marks, query_marks, marked = scratch[:11]
        part, got, sx, sy, r_own, out_own, dr = scratch[11:18]
        gate_line, up_line = scratch[18:22], scratch[22:26]
        loaded, summed = Event(), Event()

        def work():
            fetch_dr = k.local(dr_in, dr)
            fetch_dr.start()
            load = k.local(w_qkv, wq)
            load.start()
            bias[...] = jnp.zeros_like(bias)
            expand_tables(tables, cosine, sine_a, sine_b)
            mark_documents(tables, key_marks, query_marks)
            fetch_dr.wait()
            for slot in range(2):
                for half in range(2):

                    def project(at):
                        value = mm(dr[half, at, :], w_out[slot].reshape(width, cols_q)).astype(BF16)
                        full = pl.ds(pl.multiple_of(half * tokens + at.start, 256), at.size)
                        for pp in range(cols_q // 128):
                            do[slot * 2 + pp, full, :] = value[:, pp * 128 : pp * 128 + 128]

                    rows_loop(tokens, 512, project)
                k.now += 2.0
                yield k.now
                for pp in range(cols_q // 128):
                    pair = slot * 2 + pp
                    mark_keys(key, pair, key_marks, marked)
                    yield from attention_backward(
                        k, q, v, marked, query_marks, o_t, lse, do, dq_t, dk, dv, key, pair
                    )

                    def close(at):
                        cos, sin_a, sin_b = cosine[at, :], sine_a[at, :], sine_b[at, :]
                        dq = (dq_t[:, at].T * 0.125).astype(BF16).astype(F32)
                        dkk = dk[at, :].astype(BF16).astype(F32)
                        for j, value in enumerate(
                            (turn_lanes(dq, cos, -sin_a, -sin_b), turn_lanes(dkk, cos, -sin_a, -sin_b), dv[at, :])
                        ):
                            value = value.astype(BF16)
                            low = j * cols_q + pp * 128
                            dlin[slot, at, low : low + 128] = value
                            bias[slot, 0:1, low : low + 128] += jnp.sum(value.astype(F32), axis=0, keepdims=True)

                    rows_loop(length, 256, close)
                    k.now += 2.0
                    yield k.now
            load.wait()
            for half in range(2):

                def back(at):
                    full = pl.ds(pl.multiple_of(half * tokens + at.start, 256), at.size)
                    value = sum(
                        mm_nt(dlin[slot, full, j * cols_q : (j + 1) * cols_q], wq[slot, j].reshape(width, cols_q))
                        for slot in range(2)
                        for j in range(3)
                    )
                    dr[half, at, :] = value.astype(BF16)

                rows_loop(tokens, 512, back)
                k.now += 3.5
                yield k.now
            store = k.local(dr, part_h)
            store.start()
            yield k.now + 2.0
            store.wait()

        def fetch():
            copy = k.local(mixed, part)
            copy.start()
            half = tokens // 2
            loads = [k.local(resid.at[pl.ds(i * half, half)], r_own) for i in range(2)]
            pl.when(k.home)(loads[0].start)
            yield k.now + 2.0
            copy.wait()
            k.fire(loaded)
            yield summed

            @pl.when(k.home)
            def _():
                for i in range(2):
                    loads[i].wait()

                    def step(at):
                        full = pl.ds(pl.multiple_of(i * half + at.start, 16), 16)
                        out_own[full, :] = (r_own[at, :] + scatter_sum(k, part, sx, sy, full)).astype(BF16)

                    rows_loop(half, 16, step)
                    if i == 0:
                        loads[1].start()

            k.now += 2.0
            share = k.remote(out_own, block_out, k.sib)
            keep = k.local(out_own, block_out)
            share.start(k.home)
            pl.when(k.home)(keep.start)
            yield k.now + 8.0
            share.wait(k.away)
            pl.when(k.home)(keep.wait)

        going = [Event() for _ in range(2)]
        own, sib, from_dn, from_up = gate_line
        k.add(line_scatter(k, own, gate_sib, sib, from_dn, from_up, got_gate, own_part=gate_own, following=going[0], slack=8.0))
        own, sib, from_dn, from_up = up_line
        up = (own, up_sib, sib, from_dn, from_up, got_up)
        lower, upper = (0, rows // 2), (rows // 2, rows // 2)
        k.add(line_scatter(k, *up, rows=lower, own_part=up_own, ready=(going[0],), following=going[1], slack=8.0))
        k.add(line_scatter(k, *up, rows=upper, own_part=up_own, ready=(going[1],), slack=8.0))
        k.add(fetch())
        k.add(plane_scatter(k, part, got, sx, sy, far=loaded, done=summed))
        k.add(work())

    plane = (2, tokens, width)
    return call(
        body,
        [(dr, ANY), (w_out, VMEM), (w_qkv, ANY), (q, VMEM), (key, VMEM), (v, VMEM), (lse, VMEM), (o_t, VMEM)]
        + [(item, VMEM if item is tables else ANY) for item in (tables, mixed, resid) + gate + up],
        [
            (shape((2, length, 3 * cols_q), BF16), VMEM),
            (shape((2, 8, 3 * cols_q), F32), VMEM),
            (shape(plane, BF16), ANY),
            (shape((tokens, width), BF16), ANY),
            (shape((4, rows // 2, ff_q), BF16), ANY),
            (shape((4, rows, ff_q), BF16), ANY),
        ],
        [
            pltpu.VMEM(w_qkv.shape, BF16),
            pltpu.VMEM((4, length, 128), BF16),
            pltpu.VMEM((128, length), F32),
            pltpu.VMEM((length, 128), F32),
            pltpu.VMEM((length, 128), F32),
            pltpu.VMEM((length, 128), F32),
            pltpu.VMEM((length, 128), F32),
            pltpu.VMEM((length, 128), F32),
            pltpu.VMEM((2, length, 128), BF16),
            pltpu.VMEM((2, length, 128), BF16),
            pltpu.VMEM((2, length, 128), BF16),
            pltpu.VMEM(plane, BF16),
        ]
        + scatter_scratch(tokens, width)
        + [pltpu.VMEM((tokens // 2, width), F32), pltpu.VMEM((tokens, width), BF16), pltpu.VMEM(plane, BF16)]
        + [pltpu.VMEM((line, 4, rows // 2, ff_q), BF16)]
        + line_scratch(line, rows // 2, ff_q)
        + [pltpu.VMEM((line, 4, rows, ff_q), BF16)]
        + line_scratch(line, rows, ff_q),
        line,
        3,
        40 + 3 * line_sems(line),
        63,
        "attend_back_kernel",
    )


def last_kernel(line, part_h, x, gain, dr, vec_two, bias, h_one, dlin, dr_all, o, gate):
    _, tokens, width = part_h.shape
    length = 2 * tokens
    cols_q = o.shape[2]
    rows, ff_q = width // line // 4, gate[0].shape[3]
    chunk = 512

    def body(k, ins, outs, scratch):
        part_in, x, gain, dr, vec_two, bias, h_in, dlin, dr_all_in, o, gate_own, gate_sib = ins
        grad_in, vectors, got_qkv, got_out, got_gate = outs
        part, got, sx, sy, dr_own, in_own, partial, got_v, got_z, h_one, dr_all = scratch[:11]
        qkv_own, qkv_send, qkv_sib = scratch[11:14]
        qkv_rest = scratch[14:16]
        out_own, out_send, out_sib = scratch[16:19]
        out_rest = scratch[19:21]
        gate_mine, *gate_rest = scratch[21:25]
        h_turned = scratch[25]
        loaded, arrived, ready, out_there = (Event() for _ in range(4))
        qkv_there = [Event() for _ in range(3)]
        going = [Event() for _ in range(3)]

        def fetch():
            copy = k.local(part_in, part)
            copy.start()
            yield k.now + 1.0
            copy.wait()
            k.fire(loaded)

        def work():
            copies = [k.local(h_in, h_one), k.local(dr_all_in, dr_all)]
            for copy in copies:
                copy.start()
            yield k.now + 3.0
            for copy in copies:
                copy.wait()
            def turn(left, i):
                columns = left[:, :, pl.ds(pl.multiple_of(i * chunk, chunk), chunk)].reshape(length, chunk)
                return columns.astype(F32).T.astype(BF16)

            for j in range(3):

                @pl.loop(0, width // chunk)
                def _(i):
                    at = pl.ds(pl.multiple_of(i * chunk, chunk), chunk)
                    if j == 0:
                        h_turned[at, :] = turn(h_one, i)
                    for side, target in enumerate((qkv_own, qkv_send)):
                        value = mm(h_turned[at, :], dlin[side, :, j * cols_q : (j + 1) * cols_q])
                        store_rows(target, (j,), i, value.astype(BF16), rows)

                k.now += 4.5 if j == 0 else 3.0
                k.fire(qkv_there[j])
                yield k.now

            @pl.loop(0, width // chunk)
            def _(i):
                turned = turn(dr_all, i)
                for side, target in enumerate((out_own, out_send)):
                    store_rows(target, (), i, mm(turned, o[side]).astype(BF16), rows)

            k.now += 4.0
            k.fire(out_there)
            yield k.now

        def back():
            load = k.local(dr, dr_own)
            pl.when(k.home)(load.start)
            partial[...] = jnp.zeros_like(partial)
            yield arrived
            pl.when(k.home)(load.wait)

            @pl.when(k.home)
            def _():
                def step(at):
                    value = scatter_sum(k, part, sx, sy, at)
                    scaled, inv_std = norm_rows(x[at, :].astype(F32))
                    d_in = dr_own[at, :] + norm_back(value, scaled, inv_std, gain[...])
                    in_own[at, :] = d_in.astype(BF16)
                    partial[0:8, :] += fold(value * scaled)
                    partial[8:16, :] += fold(value)

                rows_loop(tokens, 16, step)

            k.now += 5.0
            k.fire(ready)
            share = k.remote(in_own, grad_in, k.sib)
            keep = k.local(in_own, grad_in)
            share.start(k.home)
            pl.when(k.home)(keep.start)
            yield k.now + 8.0
            share.wait(k.away)
            pl.when(k.home)(keep.wait)

        def reduce_vectors():
            yield ready
            vectors[...] = jnp.zeros_like(vectors)
            for i, (source, low) in enumerate(((partial, 0), (partial, 8), (vec_two, 0), (vec_two, 8))):
                vectors[i : i + 1, :] = jnp.sum(source[low : low + 8, :], axis=0, keepdims=True)
            for slot in range(2):
                tp = k.c if slot == 0 else 1 - k.c
                at = pl.ds(pl.multiple_of((tp * 4 + k.q) * cols_q, cols_q), cols_q)
                for j in range(3):
                    vectors[4 + j : 5 + j, at] = bias[slot, 0:1, j * cols_q : (j + 1) * cols_q]
            slot = 0
            for to in (k.sib, k.nx, k.ny):
                copy = k.remote(vectors, got_v.at[slot], to)
                copy.start(late=False)
                yield k.now + 4.0
                copy.wait()
                copy.gone()
                vectors[...] += got_v[slot]
                slot += 1
            spread = []
            for d in range(1, k.line):
                spread.append(k.remote(vectors, got_z.at[d - 1], k.at_line(d)))
                spread[-1].start(late=False)
            yield k.now + 6.0
            for copy in spread:
                copy.wait()
                copy.gone()
            for d in range(1, k.line):
                vectors[...] += got_z[d - 1]

        k.add(fetch())
        k.add(work())
        k.add(plane_scatter(k, part, got, sx, sy, far=loaded, done=arrived))
        k.add(back())
        k.add(reduce_vectors())
        k.add(line_scatter(k, gate_mine, gate_sib, *gate_rest, got_gate, own_part=gate_own))
        for j in range(3):
            items = [ref.at[j] for ref in (qkv_own, qkv_send, qkv_sib, *qkv_rest, got_qkv)]
            before = (going[j - 1],) if j else ()
            k.add(line_scatter(k, *items, ready=(qkv_there[j],) + before, following=going[j]))
        k.add(line_scatter(k, out_own, out_send, out_sib, *out_rest, got_out, ready=(out_there, going[2])))

    plane = (2, tokens, width)
    full_qkv, full_out = (3, line, 4, rows, cols_q), (line, 4, rows, cols_q)
    return call(
        body,
        [(part_h, ANY), (x, VMEM), (gain, VMEM), (dr, ANY), (vec_two, VMEM), (bias, VMEM), (h_one, ANY), (dlin, VMEM), (dr_all, ANY)]
        + [(o, VMEM)]
        + [(item, ANY) for item in gate],
        [(shape((tokens, width), BF16), ANY), (shape((8, width), F32), VMEM)]
        + [(shape(dims, BF16), ANY) for dims in ((3, 4, rows, cols_q), (4, rows, cols_q))]
        + [(shape((4, rows // 2, ff_q), BF16), ANY)],
        [pltpu.VMEM(plane, BF16)]
        + scatter_scratch(tokens, width)
        + [
            pltpu.VMEM((tokens, width), F32),
            pltpu.VMEM((tokens, width), BF16),
            pltpu.VMEM((16, width), F32),
            pltpu.VMEM((3, 8, width), F32),
            pltpu.VMEM((max(line - 1, 1), 8, width), F32),
            pltpu.VMEM(plane, BF16),
            pltpu.VMEM(plane, BF16),
        ]
        + [pltpu.VMEM(full_qkv, BF16), pltpu.VMEM(full_qkv, BF16)]
        + [pltpu.VMEM((3,) + piece.shape, BF16) for piece in line_scratch(line, rows, cols_q)]
        + [pltpu.VMEM(full_out, BF16), pltpu.VMEM(full_out, BF16)]
        + line_scratch(line, rows, cols_q)
        + [pltpu.VMEM((line, 4, rows // 2, ff_q), BF16)]
        + line_scratch(line, rows // 2, ff_q)
        + [pltpu.VMEM((width, length), BF16)],
        line,
        4,
        60 + 6 * line_sems(line),
        63,
        "last_kernel",
    )


def unquarter(got):
    return jnp.concatenate([got[i] for i in range(4)], axis=1).astype(F32)


def shards(
    fsdp_size,
    block_in,
    segments,
    positions,
    gain_one,
    shift_one,
    qkv_weight,
    qkv_bias,
    out_weight,
    gain_two,
    shift_two,
    gate_weight,
    up_weight,
    down_weight,
    grad_out,
):
    line = fsdp_size // 2
    seq_local, tokens, width = block_in.shape
    head_size = qkv_bias.shape[2]
    heads_tp = qkv_bias.shape[1]
    cols_tp = heads_tp * head_size
    cols_q = cols_tp // 4
    length = 2 * tokens

    fsdp = lax.axis_index("fsdp")
    ctx = lax.axis_index("ctx")
    core = lax.axis_index("tp")
    place = fsdp % 2
    quarter = place * 2 + ctx

    x = block_in.reshape(tokens, width)
    grad = grad_out.reshape(tokens, width)
    row = lax.broadcasted_iota(jnp.int32, (8, width), 0)
    gains = jnp.zeros((8, width), F32)
    for i, vector in enumerate((gain_one, shift_one, gain_two, shift_two)):
        gains = jnp.where(row == i, vector.astype(F32)[None], gains)
    lane = jnp.arange(128, dtype=jnp.int32)
    spot = lane % head_size
    half = ROT // 2
    frequency = THETA ** (-(2.0 * (spot % half).astype(F32)) / ROT)
    angle = positions.reshape(tokens, 1).astype(F32) * frequency[None]
    turned = (spot < ROT)[None]
    table = jnp.where(
        (lane < head_size)[None], jnp.where(turned, jnp.cos(angle), 1.0), jnp.where(turned, jnp.sin(angle), 0.0)
    )
    table = jnp.where((lane == 32)[None], segments.reshape(tokens, 1).astype(F32), table)
    bias = lax.dynamic_slice_in_dim(qkv_bias.reshape(3, cols_tp), quarter * cols_q, cols_q, axis=1).astype(F32)
    bias = jnp.concatenate([bias, jnp.zeros((5, cols_q), F32)], axis=0)
    qkv = qkv_weight.transpose(1, 0, 2)

    (h_one, grad_all, h_two, resid, w_qkv, w_out, w_gate, w_up, w_down, q, key, v, attn, attn_t, lse, tables, d_hid) = forward_kernel(
        line, x, gains, grad, table, bias, qkv, out_weight, gate_weight, up_weight, down_weight
    )
    mixed, d_resid, dr_all, vec_two, low_own, low_sib, high_own, high_sib, up_own, up_sib, got_down = feed_kernel(
        line, h_two, grad_all, w_gate, w_up, w_down, d_hid, resid, grad, gains[2:3]
    )
    dlin, d_bias, d_h_one, block_out, got_gate_upper, got_up = attend_back_kernel(
        line,
        dr_all,
        w_out,
        w_qkv,
        q,
        key,
        v,
        lse,
        attn_t,
        tables,
        mixed,
        resid,
        (high_own, high_sib),
        (up_own, up_sib),
    )

    d_in, vectors, got_qkv, got_out, got_gate_lower = last_kernel(
        line, d_h_one, x, gains[0:1], d_resid, vec_two, d_bias, h_one, dlin, dr_all, attn, (low_own, low_sib)
    )
    got_gate = jnp.concatenate([got_gate_lower, got_gate_upper], axis=1)

    share = fsdp * 2 + ctx
    share_size = width // (2 * fsdp_size)
    shares = lax.dynamic_slice_in_dim(vectors[:4], share * share_size, share_size, axis=1)
    bias_size = head_size // (2 * fsdp_size)
    d_bias = vectors[4:7].reshape(3, 2, heads_tp, head_size)
    d_bias = lax.dynamic_slice(d_bias, (0, core, 0, share * bias_size), (3, 1, heads_tp, bias_size))
    d_qkv = jnp.concatenate([got_qkv[:, i] for i in range(4)], axis=2).astype(F32).transpose(1, 0, 2)
    return (
        block_out.reshape(seq_local, tokens, width),
        d_in.astype(F32).reshape(seq_local, tokens, width),
        shares[0],
        shares[1],
        d_qkv,
        d_bias.reshape(3, heads_tp, bias_size),
        unquarter(got_out),
        shares[2],
        shares[3],
        unquarter(got_gate),
        unquarter(got_up),
        unquarter(got_down),
    )


def solution(mesh):
    placed = (
        P("fsdp", "ctx", None),
        P("fsdp", "ctx"),
        P("fsdp", "ctx"),
        P(),
        P(),
        P("fsdp", None, "tp"),
        P(None, "tp", None),
        P("fsdp", "tp"),
        P(),
        P(),
        P("fsdp", "tp"),
        P("fsdp", "tp"),
        P("fsdp", "tp"),
        P("fsdp", "ctx", None),
    )

    def run(*arrays):
        return shards(mesh.shape["fsdp"], *arrays)

    return jax.shard_map(
        run,
        mesh=mesh,
        in_specs=placed,
        out_specs=(
            P("fsdp", "ctx", None),
            P("fsdp", "ctx", None),
            P(("fsdp", "ctx")),
            P(("fsdp", "ctx")),
            P(("fsdp", "ctx"), None, "tp"),
            P(None, "tp", ("fsdp", "ctx")),
            P(("fsdp", "ctx"), "tp"),
            P(("fsdp", "ctx")),
            P(("fsdp", "ctx")),
            P(("fsdp", "ctx"), "tp"),
            P(("fsdp", "ctx"), "tp"),
            P(("fsdp", "ctx"), "tp"),
        ),
        check_vma=False,
    )
```
